256 devices in a mesh: fsdp: 32 (over z, y_lo, core), ctx: 8 (over x, y_hi).
Axes of the slice: x: 4, y: 4 (y_hi: 2, y_lo: 2; y = y_hi * 2 + y_lo), z: 8, core: 2. Of those that a mesh axis runs over, the one named last changes fastest.
Arguments:
- hidden: bfloat16 [32, 2048, 5120], P('fsdp', 'ctx'), may hold values from -6 to 6
- queries: bfloat16 [32, 2048, 4096], P('fsdp', 'ctx'), may hold values from -300 to 300, as said below
- norm_gain: float32 [5120], replicated, may hold values from 0.1 to 1.9
- key_gain: float32 [128], replicated, may hold values from 0.1 to 1.9
- k_weight: bfloat16 [5120, 512], P('fsdp'), may hold values from -0.078125 to 0.078125
- v_weight: bfloat16 [5120, 512], P('fsdp'), may hold values from -0.078125 to 0.078125
- segment: int32 [32, 2048], P('fsdp', 'ctx'), may hold values from 0 to 3, as said below
- position: int32 [32, 2048], P('fsdp', 'ctx'), may hold values from 0 to 8191, as said below
Outputs:
- attended: bfloat16 [32, 2048, 4096], P('fsdp', 'ctx')
The draws below stay inside these ranges and needn't reach their ends.
Inputs may be any that keep to these rules, and one draw needn't show every extreme that they name: queries keep to the stated range. `segment`: in each stretch, read in the tokens' order, rollout numbers never fall; the tokens of a stretch lie in its slots in an order that keeps 256 slots on each index of ctx, one token of every 8 consecutive ones on each. `position`: within one rollout of a stretch positions rise by one from token to token.
All inputs are finite; a program needn't handle non-finite values.
Results may differ from the reference program's by a relative error of at most 0.0075.
The reference program's roundings to bfloat16 on the way (of `normed`, `values`, `keys` and `rounded`) count: a program that leaves them out, or rounds other values in their place, can miss the bound.
Values may be sent and summed in bfloat16 or wider, within the bound.
A program may use at most 192 MiB of HBM per device.

```python
import math
import jax
import jax.numpy as jnp
from jax import lax

D = 5120
QH = 32
KVH = 4
HD = 128
TOK_DEV = 256
G = 8
LEN = 2048
STRETCHES = 32


def layout(key):

    def one_stretch(sub):
        first, second, third = jax.random.split(sub, 3)
        cuts = jnp.sort(jax.random.randint(first, (3,), 1, LEN)).astype(jnp.int32)
        places = jnp.arange(LEN, dtype=jnp.int32)
        seg_tok = jnp.sum((places[:, None] >= cuts[None, :]).astype(jnp.int32), axis=1).astype(jnp.int32)
        starts = jnp.concatenate([jnp.zeros((1,), jnp.int32), cuts])
        bases = jax.random.randint(second, (4,), 0, 8192 - LEN + 1).astype(jnp.int32)
        bases = bases.at[0].set(0)
        bases = bases.at[3].set(8191 - (LEN - 1 - starts[3]))
        pos_tok = bases[seg_tok] + places - starts[seg_tok]
        groups = LEN // TOK_DEV
        orders = jax.vmap(lambda item: jax.random.permutation(item, groups))(jax.random.split(third, TOK_DEV))
        token_of_slot = (jnp.arange(TOK_DEV, dtype=jnp.int32)[None, :] * groups + orders.T.astype(jnp.int32)).reshape(LEN)
        return (seg_tok[token_of_slot], pos_tok[token_of_slot])
    return jax.vmap(one_stretch)(jax.random.split(key, STRETCHES))


def draw_segment(key, part):
    return layout(key)[0]


def draw_position(key, part):
    return layout(key)[1]


def draw_queries(key, part):
    key = jax.random.fold_in(key, 7)
    first = jax.random.fold_in(key, 0)
    values_out = jnp.clip(jax.random.normal(first, (STRETCHES, LEN, QH, HD), jnp.float32), -6.0, 6.0)
    return values_out.reshape(STRETCHES, LEN, QH * HD).astype(jnp.bfloat16)


def block_levels(key, dims, pieces, low, high):
    level, own = 1.0, jax.random.fold_in(key, 6)
    for axis_at, shards_of in pieces:
        heights = jnp.exp(jax.random.uniform(jax.random.fold_in(own, axis_at), (shards_of,), jnp.float32, low / len(pieces), high / len(pieces)))
        level = level * jnp.repeat(heights, dims[axis_at] // shards_of).reshape([-1 if axis == axis_at else 1 for axis in range(len(dims))])
    return level


def normal_values(key, dims, scale, bound, shards=(), held_as=jnp.bfloat16):
    level = block_levels(key, dims, shards, -0.22, 0.18) if shards else 1.0
    values = jax.random.normal(key, dims, jnp.float32) * scale * level
    return jnp.minimum(jnp.maximum(values, -bound), bound).astype(held_as)


def setup_inputs(seed: int = 0) -> dict:
    arg_keys = jax.random.split(jax.random.key(seed), 9)
    hidden = normal_values(arg_keys[0], (STRETCHES, LEN, D), 1.0, 6.0, ((0, 32), (1, 8)))
    queries = draw_queries(jax.random.fold_in(arg_keys[8], 71), 0)
    norm_gain = jnp.clip(1.0 + 0.18 * jax.random.normal(arg_keys[2], (D,), jnp.float32), 0.1, 1.9)
    key_gain = jnp.clip(1.0 + 0.18 * jax.random.normal(arg_keys[3], (HD,), jnp.float32), 0.1, 1.9)
    k_weight = normal_values(arg_keys[4], (D, KVH * HD), D ** -0.5, 0.078125, ((0, 32),))
    v_weight = normal_values(arg_keys[5], (D, KVH * HD), D ** -0.5, 0.078125, ((0, 32),))
    segment = draw_segment(jax.random.fold_in(arg_keys[8], 71), 0)
    position = draw_position(jax.random.fold_in(arg_keys[8], 71), 0)
    return dict(hidden=hidden, queries=queries, norm_gain=norm_gain, key_gain=key_gain, k_weight=k_weight, v_weight=v_weight, segment=segment, position=position)


EPS = 1e-06
THETA = 1000000.0

def rotate(values_in, where):
    width = values_in.shape[-1]
    half = width // 2
    freq = jnp.exp(jnp.arange(half, dtype=jnp.float32) * (-2.0 * math.log(THETA) / width))
    angle = where.astype(jnp.float32)[:, None] * freq[None, :]
    cosine = jnp.cos(angle)[:, None, :]
    sine = jnp.sin(angle)[:, None, :]
    first = values_in[..., :half]
    second = values_in[..., half:]
    return jnp.concatenate([first * cosine - second * sine, second * cosine + first * sine], axis=-1)

def stretch(args, norm_gain, key_gain, k_weight, v_weight):
    hidden_rows, query_rows, seg_rows, pos_rows = args
    inputs = hidden_rows.astype(jnp.float32)
    normed = (inputs * lax.rsqrt(lax.optimization_barrier(jnp.mean(inputs * inputs, axis=-1, keepdims=True)) + EPS) * norm_gain).astype(jnp.bfloat16)
    key_sums = jnp.dot(normed, k_weight, preferred_element_type=jnp.float32)
    value_sums = jnp.dot(normed, v_weight, preferred_element_type=jnp.float32)
    values = value_sums.reshape(LEN, KVH, HD).astype(jnp.bfloat16)
    raw = key_sums.reshape(LEN, KVH, HD)
    normk = raw * lax.rsqrt(lax.optimization_barrier(jnp.mean(raw * raw, axis=-1, keepdims=True)) + EPS) * key_gain
    keys = rotate(normk, pos_rows).astype(jnp.bfloat16)
    block = math.gcd(LEN, 512)
    count = LEN // block
    grouped = query_rows.reshape(count, block, KVH, G, HD)
    seg_blocks = seg_rows.reshape(count, block)
    pos_blocks = pos_rows.reshape(count, block)
    scale = 1.0 / math.sqrt(HD)
    keys_wide = keys.astype(jnp.float32)
    values_wide = values.astype(jnp.float32)

    def one_block(piece):
        query_block, seg_block, pos_block = piece
        scores = jnp.einsum('tkgd,skd->kgts', query_block.astype(jnp.float32), keys_wide) * scale
        allowed = (seg_rows[None, :] == seg_block[:, None]) & (pos_rows[None, :] <= pos_block[:, None])
        scores = jnp.where(allowed, scores, -1e+30)
        top = lax.optimization_barrier(jnp.max(scores, axis=-1, keepdims=True))
        weights = jnp.where(allowed, jnp.exp(scores - top), 0.0)
        total = lax.optimization_barrier(jnp.sum(weights, axis=-1))
        rounded = weights.astype(jnp.bfloat16)
        summed = jnp.einsum('kgts,skd->kgtd', rounded.astype(jnp.float32), values_wide)
        result = summed / total[..., None]
        return jnp.transpose(result, (2, 0, 1, 3)).reshape(block, QH * HD).astype(jnp.bfloat16)
    return lax.map(one_block, (grouped, seg_blocks, pos_blocks)).reshape(LEN, QH * HD)

def reference(hidden, queries, norm_gain, key_gain, k_weight, v_weight, segment, position):
    return lax.map(lambda args: stretch(args, norm_gain, key_gain, k_weight, v_weight), (hidden, queries, segment, position))
```

```python
import functools
import math

import jax
import jax.numpy as jnp
from jax import lax
from jax.experimental import pallas as pl
from jax.experimental.pallas import tpu as pltpu
from jax.sharding import PartitionSpec as P

KVH = 4
HD = 128
G = 8
GROUPS = 8
EPS = 1e-06
THETA = 1000000.0
BIG = 8192
NEG = -1e30
X, Y, Z = 4, 4, 8
MESH = pl.DeviceIdType.MESH


def place():
    f = lax.axis_index("fsdp")
    c = lax.axis_index("ctx")
    return c // 2, (c % 2) * 2 + (f // 2) % 2, f // 4, f % 2


def device(x, y, z, core):
    x, y, z = (x + X) % X, (y + Y) % Y, (z + Z) % Z
    return {"fsdp": (z * 2 + y % 2) * 2 + core, "ctx": x * 2 + y // 2}


def gather_kernel(
    hidden_ref, gain_ref, key_gain_ref, cos_ref, sin_ref, code_ref, kw_ref, vw_ref,
    kv_ref, codes_ref,
    wbuf, normed, kv, codes,
    z_send, z_recv, y_send, y_recv, d_send, d_recv, kv_send, kv_recv, c_send, c_recv, out_sem,
):
    x, y, z, core = place()
    ylo, yhi = y % 2, y // 2
    ctx = x * 2 + yhi
    sgn = 1 - 2 * core
    rows = kw_ref.shape[0]
    width = 2 * HD
    tokens = hidden_ref.shape[0]
    half = tokens // 2

    peers = [(x + dx, y + dy, z, core) for dx in range(X) for dy in (0, 2) if (dx, dy) != (0, 0)]
    near = [(x, y, z + 1, core), (x, y, z - 1, core), (x, y + 1, z, core), (x, y - 1, z, core), (x, y, z, 1 - core)]
    barrier = pltpu.get_barrier_semaphore()
    for at in peers + near:
        pl.semaphore_signal(barrier, inc=1, device_id=device(*at), device_id_type=MESH)

    for h in range(KVH):
        wbuf[h, z, ylo, core, :, :HD] = kw_ref[:, h * HD:(h + 1) * HD]
        wbuf[h, z, ylo, core, :, HD:] = vw_ref[:, h * HD:(h + 1) * HD]
    codes[ctx] = code_ref[...]
    pl.semaphore_wait(barrier, len(peers + near))

    sent = []

    def send(src, dst, ssem, rsem, at):
        copy = pltpu.make_async_remote_copy(
            src_ref=src, dst_ref=dst, send_sem=ssem, recv_sem=rsem, device_id=device(*at), device_id_type=MESH)
        copy.start()
        sent.append(copy)

    def arrived(dst, ssem, rsem):
        pltpu.make_async_remote_copy(
            src_ref=dst, dst_ref=dst, send_sem=ssem, recv_sem=rsem, device_id=device(x, y, z, 1 - core),
            device_id_type=MESH).wait_recv()

    def slab(h, zz, yl, cc):
        return wbuf.at[h, (zz + 2 * Z) % Z, yl, cc]

    def ring(h, way, step):
        zz = z - sgn * step if way == 0 else z + sgn * step
        to = z + sgn if way == 0 else z - sgn
        block = slab(h, zz, ylo, core)
        if step > 0:
            arrived(block, z_send.at[h, way, step - 1], z_recv.at[h, way, step - 1])
        if step < (4 if way == 0 else 3):
            send(block, block, z_send.at[h, way, step], z_recv.at[h, way, step], (x, y, to, core))
        if way == 1 or step > 0:
            k = (step - 1) if way == 0 else 4 + step
            send(block, block, y_send.at[h, k], y_recv.at[h, k], (x, y + sgn if way == 0 else y - sgn, z, core))

    def w_start(h):
        ring(h, 0, 0)
        ring(h, 1, 0)

    def w_step(h, s):
        ring(h, 0, s)
        if s < 4:
            ring(h, 1, s)
        if s == 4:
            own = wbuf.at[h, :, ylo, core]
            send(own, own, d_send.at[h, 0], d_recv.at[h, 0], (x, y, z, 1 - core))

    def w_other(h):
        for k in range(8):
            zz = z - sgn * (k + 1) if k < 4 else z + sgn * (k - 4)
            arrived(slab(h, zz, 1 - ylo, core), y_send.at[h, k], y_recv.at[h, k])
        own = wbuf.at[h, :, 1 - ylo, core]
        send(own, own, d_send.at[h, 1], d_recv.at[h, 1], (x, y, z, 1 - core))

    def kv_send_to(h, n, block, at):
        send(block, block, kv_send.at[h, n], kv_recv.at[h, n], at)

    def kv_arrived(h, n, block):
        arrived(block, kv_send.at[h, n], kv_recv.at[h, n])

    def project(h):
        arrived(wbuf.at[h, :, ylo, 1 - core], d_send.at[h, 0], d_recv.at[h, 0])
        arrived(wbuf.at[h, :, 1 - ylo, 1 - core], d_send.at[h, 1], d_recv.at[h, 1])
        sums = jnp.zeros((tokens, width), jnp.float32)
        deep = 4 * rows
        for n in range(Z):
            sums += jnp.dot(normed[:, n * deep:(n + 1) * deep], wbuf[h, n].reshape(deep, width), preferred_element_type=jnp.float32)
        raw = sums[:, :HD]
        normk = raw * lax.rsqrt(jnp.mean(raw * raw, axis=-1, keepdims=True) + EPS) * key_gain_ref[...]
        turned = jnp.concatenate([normk[:, HD // 2:], normk[:, :HD // 2]], axis=1)
        kv[h, ctx, :, :HD] = (normk * cos_ref[...] + turned * sin_ref[...]).astype(jnp.bfloat16)
        kv[h, ctx, :, HD:] = sums[:, HD:].astype(jnp.bfloat16)
        block = kv.at[h, ctx]
        kv_send_to(h, 0, block, (x, y + 2, z, core))
        kv_send_to(h, 1, block, (x + 1, y, z, core))
        kv_send_to(h, 2, block, (x - 1, y, z, core))

    def spread(h, yh, base):
        left = ((x + X - 1) % X) * 2 + yh
        right = ((x + 1) % X) * 2 + yh
        kv_arrived(h, base, kv.at[h, left])
        kv_send_to(h, base + 2, kv.at[h, left, pl.ds(0, half)], (x + 1, y, z, core))
        kv_arrived(h, base + 1, kv.at[h, right])
        kv_send_to(h, base + 3, kv.at[h, right, pl.ds(half, half)], (x - 1, y, z, core))

    def kv_first(h):
        other = kv.at[h, x * 2 + 1 - yhi]
        kv_arrived(h, 0, other)
        kv_send_to(h, 5, other, (x + 1, y, z, core))
        kv_send_to(h, 6, other, (x - 1, y, z, core))
        spread(h, yhi, 1)

    def kv_second(h):
        spread(h, 1 - yhi, 5)

    def kv_last(h):
        far = ((x + 2) % X) * 2
        for yh, base in ((yhi, 1), (1 - yhi, 5)):
            kv_arrived(h, base + 2, kv.at[h, far + yh, pl.ds(0, half)])
            kv_arrived(h, base + 3, kv.at[h, far + yh, pl.ds(half, half)])
        out = pltpu.make_async_copy(kv.at[h], kv_ref.at[h], out_sem.at[h])
        out.start()
        outs.append(out)

    outs = []
    w_start(0)
    for n, at in enumerate(peers):
        send(codes.at[ctx], codes.at[ctx], c_send.at[n], c_recv.at[n], at)

    @pl.loop(0, tokens // 32)
    def _(n):
        part = pl.ds(pl.multiple_of(n * 32, 32), 32)
        wide = hidden_ref[part, :].astype(jnp.float32)
        scale = lax.rsqrt(jnp.mean(wide * wide, axis=-1, keepdims=True) + EPS)
        normed[part, :] = (wide * scale * gain_ref[...]).astype(jnp.bfloat16)

    w_step(0, 1); w_step(0, 2); w_step(0, 3)
    w_start(1)
    w_step(0, 4)
    w_step(1, 1)
    w_other(0)
    w_step(1, 2)
    project(0)
    w_step(1, 3)
    w_start(2)
    w_step(1, 4)
    w_step(2, 1)
    kv_first(0)
    w_other(1)
    w_step(2, 2)
    project(1)
    w_step(2, 3)
    w_start(3)
    kv_second(0)
    w_step(2, 4)
    w_step(3, 1)
    kv_first(1)
    w_other(2)
    w_step(3, 2)
    project(2)
    w_step(3, 3)
    kv_second(1)
    kv_last(0)
    w_step(3, 4)
    w_other(3)
    kv_first(2)
    project(3)
    kv_last(1)
    kv_second(2)
    kv_first(3)
    kv_last(2)
    kv_second(3)
    for n, (px, py, _, _) in enumerate(peers):
        dx, dy = [(dx, dy) for dx in range(X) for dy in (0, 2) if (dx, dy) != (0, 0)][n]
        src = ((x + X - dx) % X) * 2 + (yhi + dy // 2) % 2
        arrived(codes.at[src], c_send.at[n], c_recv.at[n])
    out = pltpu.make_async_copy(codes, codes_ref, out_sem.at[KVH])
    out.start()
    outs.append(out)
    kv_last(3)
    for copy in sent:
        copy.wait_send()
    for out in outs:
        out.wait()


def gather(hidden, norm_gain, key_gain, cos, sin, code, k_weight, v_weight):
    tokens, features = hidden.shape
    rows = k_weight.shape[0]
    vm = pl.BlockSpec(memory_space=pltpu.VMEM)
    dma = pltpu.SemaphoreType.DMA
    return pl.pallas_call(
        gather_kernel,
        out_shape=(jax.ShapeDtypeStruct((KVH, X * 2, tokens, 2 * HD), jnp.bfloat16), jax.ShapeDtypeStruct((X * 2, 1, tokens), jnp.int32)),
        in_specs=[vm] * 8,
        out_specs=(pl.BlockSpec(memory_space=pl.ANY), pl.BlockSpec(memory_space=pl.ANY)),
        scratch_shapes=[
            pltpu.VMEM((KVH, Z, 2, 2, rows, 2 * HD), jnp.bfloat16),
            pltpu.VMEM((tokens, features), jnp.bfloat16),
            pltpu.VMEM((KVH, X * 2, tokens, 2 * HD), jnp.bfloat16),
            pltpu.VMEM((X * 2, 1, tokens), jnp.int32),
            dma((KVH, 2, 4)), dma((KVH, 2, 4)), dma((KVH, 8)), dma((KVH, 8)), dma((KVH, 2)), dma((KVH, 2)),
            dma((KVH, 9)), dma((KVH, 9)), dma((7,)), dma((7,)), dma((KVH + 1,)),
        ],
        compiler_params=pltpu.CompilerParams(collective_id=0, has_side_effects=True, vmem_limit_bytes=50 * 2**20),
        cost_estimate=pl.CostEstimate(flops=3 * 10**9, bytes_accessed=10**8, transcendentals=0),
        name="project_and_gather",
    )(hidden, norm_gain, key_gain, cos, sin, code, k_weight, v_weight)


def attend_kernel(rows, q_ref, kv_ref, key_code_ref, own_code_ref, o_ref, s_ref, acc_ref, den_ref, lim_ref):
    tiles = key_code_ref.shape[0]
    slots = rows // tiles
    keys_in = GROUPS * slots
    shift = math.log2(math.e) / math.sqrt(HD)
    kc = key_code_ref[...]
    k_min = jnp.min(kc, axis=1, keepdims=True)
    k_max = jnp.max(kc, axis=1, keepdims=True)
    lim_ref[...] = jnp.concatenate([k_min, k_max] + [jnp.zeros((tiles, 126), jnp.int32)], axis=1)

    def one_tile(i, _):
        base = pl.multiple_of(i * slots, slots)
        own = own_code_ref[pl.ds(base, slots), :]
        start = (own // BIG) * BIG
        q_max = jnp.max(own)
        q_low = jnp.min(start)
        qs = []
        for k in range(KVH):
            blk = q_ref[pl.ds(base, slots), k * G * HD:(k + 1) * G * HD]
            qs.append(jnp.concatenate([blk[:, g * HD:(g + 1) * HD] for g in range(G)], axis=0))
        active = (k_min <= q_max) & (k_max >= q_low)
        where = lax.broadcasted_iota(jnp.int32, (tiles, 1), 0)
        first = jnp.min(jnp.where(active, where, tiles))
        last = jnp.max(jnp.where(active, where, -1))

        def scores(j, tops):
            codes = key_code_ref[pl.ds(j, 1), :]
            allowed = (codes <= own) & (codes >= start)
            bias = jnp.where(allowed, jnp.float32(3e38), jnp.float32(NEG))
            out = []
            for k in range(KVH):
                kt = kv_ref[k, :, pl.ds(pl.multiple_of(j * slots, slots), slots), :HD].reshape(keys_in, HD)
                s = lax.dot_general(qs[k], kt, (((1,), (1,)), ((), ())), preferred_element_type=jnp.float32)
                s = jnp.minimum(s.reshape(G, slots, keys_in), bias[None]).reshape(G * slots, keys_in)
                s_ref[k, j] = s
                out.append(jnp.maximum(tops[k], jnp.maximum(s[:, :HD], s[:, HD:])))
            return tuple(out)

        tops = lax.fori_loop(first, last + 1, scores, tuple(jnp.full((G * slots, HD), NEG, jnp.float32) for _ in range(KVH)))
        tops = [jnp.max(t, axis=1, keepdims=True) * shift for t in tops]
        acc_ref[...] = jnp.zeros_like(acc_ref)
        den_ref[...] = jnp.zeros_like(den_ref)

        def weigh(j, _):
            for k in range(KVH):
                vt = kv_ref[k, :, pl.ds(pl.multiple_of(j * slots, slots), slots), HD:].reshape(keys_in, HD)
                w = jnp.exp2(s_ref[k, j] * shift - tops[k])
                den_ref[k] += w[:, :HD] + w[:, HD:]
                acc_ref[k] += jnp.dot(w.astype(jnp.bfloat16), vt, preferred_element_type=jnp.float32)
            return 0

        lax.fori_loop(first, last + 1, weigh, 0)
        for k in range(KVH):
            total = jnp.sum(den_ref[k], axis=1, keepdims=True)
            res = (acc_ref[k] / total).astype(jnp.bfloat16)
            for g in range(G):
                o_ref[pl.ds(base, slots), (k * G + g) * HD:(k * G + g + 1) * HD] = res[g * slots:(g + 1) * slots]
        return 0

    lax.fori_loop(0, tiles, one_tile, 0)

def attend(queries, kv, key_code, own_code):
    rows = queries.shape[0]
    tiles = key_code.shape[0]
    slots = rows // tiles
    m = G * slots
    vm = pl.BlockSpec(memory_space=pltpu.VMEM)
    return pl.pallas_call(
        functools.partial(attend_kernel, rows),
        out_shape=jax.ShapeDtypeStruct(queries.shape, jnp.bfloat16),
        in_specs=[vm] * 4, out_specs=vm,
        scratch_shapes=[pltpu.VMEM((KVH, tiles, m, GROUPS * slots), jnp.float32), pltpu.VMEM((KVH, m, HD), jnp.float32),
                        pltpu.VMEM((KVH, m, HD), jnp.float32), pltpu.VMEM((tiles, 128), jnp.int32)],
        compiler_params=pltpu.CompilerParams(vmem_limit_bytes=48 * 2**20),
        cost_estimate=pl.CostEstimate(flops=10**10, bytes_accessed=10**7, transcendentals=10**7),
        name="attend",
    )(queries, kv, key_code, own_code)


def on_device(hidden, queries, norm_gain, key_gain, k_weight, v_weight, segment, position):
    tokens = hidden.shape[1]
    half = HD // 2
    freq = jnp.exp(jnp.arange(half, dtype=jnp.float32) * (-2.0 * math.log(THETA) / HD))
    angle = position[0].astype(jnp.float32)[:, None] * freq[None, :]
    cosine, sine = jnp.cos(angle), jnp.sin(angle)
    code = segment * BIG + position
    kv, codes = gather(
        hidden[0], norm_gain[None], key_gain[None], jnp.concatenate([cosine, cosine], axis=1),
        jnp.concatenate([-sine, sine], axis=1), code, k_weight, v_weight)
    tiles = 8
    key_code = codes.reshape(GROUPS, tiles, tokens // tiles).transpose(1, 0, 2).reshape(tiles, -1)
    return attend(queries[0], kv, key_code, code.reshape(tokens, 1))[None]


def solution(mesh):
    placed = (
        P("fsdp", "ctx", None),
        P("fsdp", "ctx", None),
        P(),
        P(),
        P("fsdp", None),
        P("fsdp", None),
        P("fsdp", "ctx"),
        P("fsdp", "ctx"),
    )
    return jax.shard_map(
        on_device, mesh=mesh, in_specs=placed, out_specs=P("fsdp", "ctx", None), check_vma=False
    )
```

```python
import functools
import math

import jax
import jax.numpy as jnp
from jax import lax
from jax.experimental import pallas as pl
from jax.experimental.pallas import tpu as pltpu
from jax.sharding import PartitionSpec as P

KVH = 4
HD = 128
G = 8
GROUPS = 8
EPS = 1e-06
THETA = 1000000.0
BIG = 8192
NEG = -1e30
X, Y, Z = 4, 4, 8
TILES = 4
MESH = pl.DeviceIdType.MESH


def place():
    f = lax.axis_index("fsdp")
    c = lax.axis_index("ctx")
    return c // 2, (c % 2) * 2 + (f // 2) % 2, f // 4, f % 2


def device(x, y, z, core):
    x, y, z = (x + X) % X, (y + Y) % Y, (z + Z) % Z
    return {"fsdp": (z * 2 + y % 2) * 2 + core, "ctx": x * 2 + y // 2}


ORDER = (
    "z000", "z300", "z310", "r", "h0", "z010", "z001", "z210", "z301", "m", "z011", "z100", "z211", "z002", "z012",
    "h1", "z302", "h3", "z200", "z311", "z013", "z003", "n", "z303", "z312", "z101", "z201", "z004", "z110", "E0",
    "z304", "z212", "z313", "h2", "o0", "o3", "E3", "f0", "z102", "z202", "p0", "f3", "z111", "z213", "z103", "p3",
    "z203", "K00", "o2", "z112", "L0", "o1", "K01", "z204", "z104", "z113", "K30", "K31", "E2", "f2", "q", "M00",
    "E1", "M01", "L3", "Q0", "f1", "p2", "Q3", "p1", "N0", "A00", "A01", "K20", "K21", "A02", "M31", "M30", "L2",
    "A03", "N3", "A30", "Q2", "K11", "K10", "A31", "A32", "A33", "L1", "Q1", "M20", "M21", "N2", "A20", "A21",
    "A22", "A23", "M10", "M11", "N1", "A10", "A11", "A12", "A13",
)
BY_Y = (0, 1, 2, 3)
ALL_Y = (0,)


def fused_kernel(
    hidden_hbm, queries_hbm, gain_hbm, key_gain_hbm, segment_hbm, position_hbm, kw_hbm, vw_hbm,
    out_hbm,
    hidden, queries, gain_ref, key_gain_ref, segment_ref, position_ref, kw, vw, wbuf, normed, kv, codes, perm, perm_t, cos, sin, own_code, bias, held, rows_out, out,
    in_sem, z_send, z_recv, o_send, o_recv, h_send, h_recv, y_send, y_recv, d_send, d_recv,
    kv_send, kv_recv, c_send, c_recv, out_sem,
):
    x, y, z, core = place()
    ylo, yhi = y % 2, y // 2
    ctx = x * 2 + yhi
    sgn = 1 - 2 * core
    rows = kw.shape[0]
    width = 2 * HD
    tokens = hidden.shape[0]
    half = tokens // 2
    slots = tokens // TILES
    m, keys_in = G * slots, GROUPS * slots
    shift = math.log2(math.e) / math.sqrt(HD)

    loads = [pltpu.make_async_copy(a, b, in_sem.at[n]) for n, (a, b) in enumerate(((kw_hbm, kw), (vw_hbm, vw), (segment_hbm, segment_ref), (position_hbm, position_ref), (key_gain_hbm, key_gain_ref), (gain_hbm, gain_ref), (hidden_hbm, hidden), (queries_hbm, queries)))]
    for load in loads:
        load.start()
    peers = [(x + dx, y + dy, z, core) for dx in range(X) for dy in (0, 2) if (dx, dy) != (0, 0)]
    near = [(x, y, z + 1, core), (x, y, z - 1, core), (x, y + 1, z, core), (x, y - 1, z, core), (x, y, z, 1 - core)]
    barrier = pltpu.get_barrier_semaphore()
    for at in near + peers:
        pl.semaphore_signal(barrier, inc=1, device_id=device(*at), device_id_type=MESH)
    loads[0].wait()
    loads[1].wait()
    for h in range(KVH):
        wbuf[h, z, ylo, core, :, :HD] = kw[:, h * HD:(h + 1) * HD]
        wbuf[h, z, ylo, core, :, HD:] = vw[:, h * HD:(h + 1) * HD]
    pl.semaphore_wait(barrier, len(peers + near))

    sent = []
    outs = []

    def send(src, dst, ssem, rsem, at):
        copy = pltpu.make_async_remote_copy(
            src_ref=src, dst_ref=dst, send_sem=ssem, recv_sem=rsem, device_id=device(*at), device_id_type=MESH)
        copy.start()
        sent.append(copy)

    def arrived(dst, ssem, rsem):
        pltpu.make_async_remote_copy(
            src_ref=dst, dst_ref=dst, send_sem=ssem, recv_sem=rsem, device_id=device(x, y, z, 1 - core),
            device_id_type=MESH).wait_recv()

    def slab(h, zz, yl):
        return wbuf.at[h, (zz + 2 * Z) % Z, yl, core]

    def ring(h, way, step):
        way_z = -sgn if way == 0 else sgn
        block = slab(h, z + way_z * step, ylo)
        if step > 0:
            arrived(block, z_send.at[h, way, step - 1], z_recv.at[h, way, step - 1])
        if step < (4 if way == 0 else 3):
            send(block, block, z_send.at[h, way, step], z_recv.at[h, way, step], (x, y, z - way_z, core))
        if step > (0 if h in ALL_Y else 1):
            send(block, block, y_send.at[h, way, step - 1], y_recv.at[h, way, step - 1], (x, y - way_z, z, core))

    def halves(h, zz, yl):
        block = slab(h, zz, yl)
        return block.at[pl.ds(0, rows // 2)], block.at[pl.ds(rows // 2, rows // 2)]

    def cross(h):
        low, high = halves(h, z, ylo)
        send(low, low, h_send.at[h, 0], h_recv.at[h, 0], (x, y + 1, z, core))
        send(high, high, h_send.at[h, 1], h_recv.at[h, 1], (x, y - 1, z, core))

    def crossed(h):
        low, high = halves(h, z, 1 - ylo)
        arrived(low, h_send.at[h, 0], h_recv.at[h, 0])
        arrived(high, h_send.at[h, 1], h_recv.at[h, 1])
        if h not in ALL_Y:
            block = slab(h, z, 1 - ylo)
            send(block, block, o_send.at[h, 0], o_recv.at[h, 0], (x, y, z + 1, core))
            send(block, block, o_send.at[h, 1], o_recv.at[h, 1], (x, y, z - 1, core))

    def share_own(h):
        own = wbuf.at[h, :, ylo, core]
        send(own, own, d_send.at[h, 0], d_recv.at[h, 0], (x, y, z, 1 - core))

    def share_other(h):
        if h not in ALL_Y:
            arrived(slab(h, z - 1, 1 - ylo), o_send.at[h, 0], o_recv.at[h, 0])
            arrived(slab(h, z + 1, 1 - ylo), o_send.at[h, 1], o_recv.at[h, 1])
        for way in (0, 1):
            way_z = -sgn if way == 0 else sgn
            for k in range(0 if h in ALL_Y else 1, 4 - way):
                arrived(slab(h, z + way_z * (k + 1), 1 - ylo), y_send.at[h, way, k], y_recv.at[h, way, k])
        own = wbuf.at[h, :, 1 - ylo, core]
        send(own, own, d_send.at[h, 1], d_recv.at[h, 1], (x, y, z, 1 - core))

    def kv_send_to(h, n, block, at):
        send(block, block, kv_send.at[h, n], kv_recv.at[h, n], at)

    def kv_arrived(h, n, block):
        arrived(block, kv_send.at[h, n], kv_recv.at[h, n])

    def project(h):
        arrived(wbuf.at[h, :, ylo, 1 - core], d_send.at[h, 0], d_recv.at[h, 0])
        arrived(wbuf.at[h, :, 1 - ylo, 1 - core], d_send.at[h, 1], d_recv.at[h, 1])
        sums = jnp.zeros((tokens, width), jnp.float32)
        deep = 4 * rows
        for n in range(Z):
            sums += jnp.dot(normed[:, n * deep:(n + 1) * deep], wbuf[h, n].reshape(deep, width), preferred_element_type=jnp.float32)
        raw = sums[:, :HD]
        normk = raw * lax.rsqrt(jnp.mean(raw * raw, axis=-1, keepdims=True) + EPS) * key_gain_ref[...]
        turned = jnp.concatenate([normk[:, HD // 2:], normk[:, :HD // 2]], axis=1)
        keys = (normk * cos[...] + turned * sin[...]).astype(jnp.bfloat16)
        both = jnp.concatenate([keys, sums[:, HD:].astype(jnp.bfloat16)], axis=1)
        kv[h, ctx] = jnp.dot(perm[...], both, preferred_element_type=jnp.float32).astype(jnp.bfloat16)
        block = kv.at[h, ctx]
        kv_send_to(h, 0, block, (x, y + 2, z, core))
        kv_send_to(h, 1, block, (x + 1, y, z, core))
        kv_send_to(h, 2, block, (x - 1, y, z, core))

    def spread(h, yh, base, side):
        step = 1 if side == 0 else -1
        block = kv.at[h, ((x - step + X) % X) * 2 + yh]
        kv_arrived(h, base + side, block)
        if base == 1 or h not in BY_Y:
            part = block.at[pl.ds(side * half, half)]
            kv_send_to(h, base + 2 + side, part, (x + step, y, z, core))

    def kv_partner(h):
        other = kv.at[h, x * 2 + 1 - yhi]
        kv_arrived(h, 0, other)
        kv_send_to(h, 5, other, (x + 1, y, z, core))
        kv_send_to(h, 6, other, (x - 1, y, z, core))

    def far(h, yh):
        return kv.at[h, ((x + 2) % X) * 2 + yh]

    def kv_far(h):
        for side in (0, 1):
            kv_arrived(h, 3 + side, far(h, yhi).at[pl.ds(side * half, half)])
        if h in BY_Y:
            kv_send_to(h, 9, far(h, yhi), (x, y + 2, z, core))

    def kv_last(h):
        if h in BY_Y:
            kv_arrived(h, 9, far(h, 1 - yhi))
        else:
            for side in (0, 1):
                kv_arrived(h, 7 + side, far(h, 1 - yhi).at[pl.ds(side * half, half)])

    def order():
        shape = (tokens, tokens)
        down, across = lax.broadcasted_iota(jnp.int32, shape, 0), lax.broadcasted_iota(jnp.int32, shape, 1)
        same = down == across

        def column(row):
            return jnp.sum(jnp.where(same, row, 0.0), axis=1, keepdims=True)

        for load in loads[2:5]:
            load.wait()
        where = position_ref[...].astype(jnp.float32)
        row = (segment_ref[...] * BIG + position_ref[...]).astype(jnp.float32)
        col = column(row)
        rank_row = jnp.sum(jnp.where(col < row, 1.0, 0.0), axis=0, keepdims=True)
        rank_col = jnp.sum(jnp.where(row < col, 1.0, 0.0), axis=1, keepdims=True)
        put = rank_row == down.astype(jnp.float32)
        take = rank_col == across.astype(jnp.float32)
        perm[...] = jnp.where(put, 1.0, 0.0).astype(jnp.bfloat16)
        perm_t[...] = jnp.where(take, 1.0, 0.0).astype(jnp.bfloat16)
        codes[ctx] = jnp.sum(jnp.where(take, col, 0.0), axis=0, keepdims=True).astype(jnp.int32)
        own_code[...] = jnp.broadcast_to(jnp.sum(jnp.where(put, row, 0.0), axis=1, keepdims=True), (tokens, HD)).astype(jnp.int32)
        for n, at in enumerate(peers):
            send(codes.at[ctx], codes.at[ctx], c_send.at[n], c_recv.at[n], at)
        lane = lax.broadcasted_iota(jnp.int32, (1, HD), 1)
        freq = jnp.exp((lane % (HD // 2)).astype(jnp.float32) * (-2.0 * math.log(THETA) / HD))
        angle = column(where) * freq
        cos[...] = jnp.cos(angle)
        sin[...] = jnp.where(lane < HD // 2, -1.0, 1.0) * jnp.sin(angle)

    def masks():
        for n in range(len(peers)):
            dx, dy = [(dx, dy) for dx in range(X) for dy in (0, 2) if (dx, dy) != (0, 0)][n]
            src = ((x + X - dx) % X) * 2 + (yhi + dy // 2) % 2
            arrived(codes.at[src], c_send.at[n], c_recv.at[n])
        own = own_code[:, :1]
        start = own // BIG * BIG
        for j in range(TILES):
            there = jnp.concatenate([codes[d, :, j * slots:(j + 1) * slots] for d in range(GROUPS)], axis=1)
            bias[j] = jnp.where((there <= own) & (there >= start), jnp.float32(3e38), jnp.float32(NEG))

    def sort_queries():
        loads[7].wait()
        for h in range(KVH):
            part = pl.ds(h * G * HD, G * HD)
            queries[:, part] = jnp.dot(perm[...], queries[:, part], preferred_element_type=jnp.float32).astype(jnp.bfloat16)

    def attend(h, i):
        blk = queries[i * slots:(i + 1) * slots, h * G * HD:(h + 1) * G * HD]
        q = jnp.concatenate([blk[:, g * HD:(g + 1) * HD] for g in range(G)], axis=0)

        def tiles(lanes):
            parts = [kv[h, :, j * slots:(j + 1) * slots, lanes].reshape(keys_in, HD) for j in range(i + 1)]
            return jnp.concatenate(parts, axis=0)

        s = lax.dot_general(q, tiles(slice(0, HD)), (((1,), (1,)), ((), ())), preferred_element_type=jnp.float32)
        top = None
        for j in range(i + 1):
            t = s[:, j * keys_in:(j + 1) * keys_in].reshape(G, slots, keys_in)
            t = jnp.minimum(t, bias[j, i * slots:(i + 1) * slots, :][None]).reshape(m, keys_in)
            held[j] = t
            most = jnp.maximum(jnp.maximum(t[:, :HD], t[:, HD:2 * HD]), jnp.maximum(t[:, 2 * HD:3 * HD], t[:, 3 * HD:]))
            top = most if top is None else jnp.maximum(top, most)
        low = jnp.max(top, axis=1, keepdims=True) * shift
        w = jnp.concatenate([jnp.exp2(held[j] * shift - low).astype(jnp.bfloat16) for j in range(i + 1)], axis=1)
        value = tiles(slice(HD, 2 * HD))
        acc = jnp.dot(w, jnp.concatenate([value, jnp.ones_like(value)], axis=1), preferred_element_type=jnp.float32)
        res = (acc[:, :HD] / acc[:, HD:]).astype(jnp.bfloat16)
        part = pl.ds(i * slots, slots)
        rows_out[part, :] = jnp.concatenate([res[g * slots:(g + 1) * slots] for g in range(G)], axis=1)
        if i == TILES - 1:
            out[h] = jnp.dot(perm_t[...], rows_out[...], preferred_element_type=jnp.float32).astype(jnp.bfloat16)
            copy = pltpu.make_async_copy(out.at[h], out_hbm.at[:, pl.ds(h * G * HD, G * HD)], out_sem.at[h])
            copy.start()
            outs.append(copy)

    def norm():
        loads[5].wait()
        loads[6].wait()

        @pl.loop(0, tokens // 32)
        def _(n):
            part = pl.ds(pl.multiple_of(n * 32, 32), 32)
            wide = hidden[part, :].astype(jnp.float32)
            scale = lax.rsqrt(jnp.mean(wide * wide, axis=-1, keepdims=True) + EPS)
            normed[part, :] = (wide * scale * gain_ref[...]).astype(jnp.bfloat16)

    steps = {
        "z": ring, "h": cross, "o": crossed, "E": share_own, "f": share_other, "p": project,
        "K": lambda h, side: spread(h, yhi, 1, side), "L": kv_partner,
        "M": lambda h, side: spread(h, 1 - yhi, 5, side), "Q": kv_far, "N": kv_last, "A": attend,
    }
    plain = {"n": norm, "r": order, "m": masks, "q": sort_queries}
    for item in ORDER:
        if item in plain:
            plain[item]()
        else:
            steps[item[0]](*[int(digit) for digit in item[1:]])
    for copy in sent:
        copy.wait_send()
    for out in outs:
        out.wait()


def fused(hidden, queries, norm_gain, key_gain, segment, position, k_weight, v_weight):
    tokens, features = hidden.shape
    rows = k_weight.shape[0]
    slots = tokens // TILES
    m, keys_in = G * slots, GROUPS * slots
    hbm = pl.BlockSpec(memory_space=pl.ANY)
    dma = pltpu.SemaphoreType.DMA
    half, full = jnp.bfloat16, jnp.float32
    return pl.pallas_call(
        fused_kernel,
        out_shape=jax.ShapeDtypeStruct(queries.shape, half),
        in_specs=[hbm] * 8,
        out_specs=hbm,
        scratch_shapes=[
            pltpu.VMEM((tokens, features), half),
            pltpu.VMEM(queries.shape, half),
            pltpu.VMEM(norm_gain.shape, full),
            pltpu.VMEM(key_gain.shape, full),
            pltpu.VMEM(segment.shape, jnp.int32),
            pltpu.VMEM(position.shape, jnp.int32),
            pltpu.VMEM(k_weight.shape, half),
            pltpu.VMEM(v_weight.shape, half),
            pltpu.VMEM((KVH, Z, 2, 2, rows, 2 * HD), half),
            pltpu.VMEM((tokens, features), half),
            pltpu.VMEM((KVH, GROUPS, tokens, 2 * HD), half),
            pltpu.VMEM((GROUPS, 1, tokens), jnp.int32),
            pltpu.VMEM((tokens, tokens), half),
            pltpu.VMEM((tokens, tokens), half),
            pltpu.VMEM((tokens, HD), full),
            pltpu.VMEM((tokens, HD), full),
            pltpu.VMEM((tokens, HD), jnp.int32),
            pltpu.VMEM((TILES, tokens, keys_in), full),
            pltpu.VMEM((TILES, m, keys_in), full),
            pltpu.VMEM((tokens, G * HD), half),
            pltpu.VMEM((KVH, tokens, G * HD), half),
            dma((8,)),
            dma((KVH, 2, 4)), dma((KVH, 2, 4)), dma((KVH, 2)), dma((KVH, 2)), dma((KVH, 2)), dma((KVH, 2)),
            dma((KVH, 2, 4)), dma((KVH, 2, 4)), dma((KVH, 2)), dma((KVH, 2)),
            dma((KVH, 10)), dma((KVH, 10)), dma((7,)), dma((7,)), dma((KVH,)),
        ],
        compiler_params=pltpu.CompilerParams(collective_id=0, has_side_effects=True, vmem_limit_bytes=60 * 2**20),
        cost_estimate=pl.CostEstimate(flops=12 * 10**9, bytes_accessed=10**8, transcendentals=2 * 10**7),
        name="project_gather_attend",
    )(hidden, queries, norm_gain, key_gain, segment, position, k_weight, v_weight)


def on_device(hidden, queries, norm_gain, key_gain, k_weight, v_weight, segment, position):
    return fused(hidden[0], queries[0], norm_gain[None], key_gain[None], segment, position, k_weight, v_weight)[None]


def solution(mesh):
    placed = (
        P("fsdp", "ctx", None),
        P("fsdp", "ctx", None),
        P(),
        P(),
        P("fsdp", None),
        P("fsdp", None),
        P("fsdp", "ctx"),
        P("fsdp", "ctx"),
    )
    return jax.shard_map(
        on_device, mesh=mesh, in_specs=placed, out_specs=P("fsdp", "ctx", None), check_vma=False
    )
```

```python
import functools
import math

import jax
import jax.numpy as jnp
from jax import lax
from jax.experimental import pallas as pl
from jax.experimental.pallas import tpu as pltpu
from jax.sharding import PartitionSpec as P

KVH = 4
HD = 128
G = 8
GROUPS = 8
EPS = 1e-06
THETA = 1000000.0
BIG = 8192
NEG = -1e30
X, Y, Z = 4, 4, 8
TILES = 4
MESH = pl.DeviceIdType.MESH


def place():
    f = lax.axis_index("fsdp")
    c = lax.axis_index("ctx")
    return c // 2, (c % 2) * 2 + (f // 2) % 2, f // 4, f % 2


def device(x, y, z, core):
    x, y, z = (x + X) % X, (y + Y) % Y, (z + Z) % Z
    return {"fsdp": (z * 2 + y % 2) * 2 + core, "ctx": x * 2 + y // 2}


ORDER = (
    "z100", "z110", "z200", "z210", "h2", "z000", "h1", "h4", "z010", "h0", "z310", "z101", "o1", "z201", "h3",
    "z111", "z001", "r", "z102", "z211", "q", "z410", "z011", "o0", "z300", "z002", "z112", "z103", "z202", "z212",
    "m", "n", "z012", "z104", "z113", "z003", "z301", "z203", "z013", "z400", "E1", "z411", "z311", "f1", "z004",
    "z213", "z302", "E0", "z412", "p1", "z312", "f0", "z401", "z204", "o2", "p0", "z303", "o4", "z313", "E2", "o3",
    "L1", "f2", "z413", "K11", "K00", "z304", "K10", "K01", "z402", "E3", "p2", "M10", "M11", "z403", "f3", "Q0",
    "Q1", "L0", "K21", "z404", "K20", "p3", "M00", "L2", "M01", "Q2", "E4", "N0", "S00", "S01", "S02", "S03", "N1",
    "V00", "f4", "V01", "K31", "K30", "S11", "S10", "p4", "V02", "V03", "M20", "M21", "L3", "Q3", "S13", "N2",
    "V10", "K40", "K41", "V11", "S12", "S20", "V12", "V13", "S21", "L4", "M31", "S23", "M30", "Q4", "N3", "V20",
    "V21", "S22", "V22", "S31", "V23", "M40", "S32", "M41", "S30", "N4", "S33", "V30", "V31", "V32", "V33",
)
PARTS = KVH + 1
BY_Y = (0, 1, 2, 3, 4)
ALL_Y = (0, 1, 2)


def fused_kernel(
    hidden_hbm, queries_hbm, gain_hbm, key_gain_hbm, segment_hbm, position_hbm, kw_hbm, vw_hbm,
    out_hbm,
    hidden, queries, gain_ref, key_gain_ref, segment_ref, position_ref, kw, vw, w_edge, w_mid, normed, kv_edge, kv_mid,
    codes, perm, perm_t, cos, sin, own_code, bias, held, tops, rows_out, out,
    in_sem, z_send, z_recv, o_send, o_recv, h_send, h_recv, y_send, y_recv, d_send, d_recv,
    kv_send, kv_recv, c_send, c_recv, out_sem,
):
    x, y, z, core = place()
    ylo, yhi = y % 2, y // 2
    ctx = x * 2 + yhi
    sgn = 1 - 2 * core
    rows = kw.shape[0]
    wbuf = [w_edge.at[0]] + [w_mid.at[n] for n in range(KVH - 1)] + [w_edge.at[1]]
    kv = [kv_edge.at[0]] + [kv_mid.at[n] for n in range(KVH - 1)] + [kv_edge.at[1]]
    tokens = hidden.shape[0]
    half = tokens // 2
    slots = tokens // TILES
    m, keys_in = G * slots, GROUPS * slots
    shift = math.log2(math.e) / math.sqrt(HD)

    loads = [pltpu.make_async_copy(a, b, in_sem.at[n]) for n, (a, b) in enumerate(((kw_hbm, kw), (vw_hbm, vw), (segment_hbm, segment_ref), (position_hbm, position_ref), (key_gain_hbm, key_gain_ref), (gain_hbm, gain_ref), (hidden_hbm, hidden), (queries_hbm, queries)))]
    for load in loads:
        load.start()
    peers = [(x + dx, y + dy, z, core) for dx in range(X) for dy in (0, 2) if (dx, dy) != (0, 0)]
    near = [(x, y, z + 1, core), (x, y, z - 1, core), (x, y + 1, z, core), (x, y - 1, z, core), (x, y, z, 1 - core)]
    barrier = pltpu.get_barrier_semaphore()
    for at in near + peers:
        pl.semaphore_signal(barrier, inc=1, device_id=device(*at), device_id_type=MESH)
    loads[0].wait()
    loads[1].wait()
    for h in range(PARTS):
        if h > 0:
            wbuf[h][z, ylo, core, :, :HD] = vw[:, (h - 1) * HD:h * HD]
        if h < KVH:
            lanes = slice(0, HD) if h == 0 else slice(HD, 2 * HD)
            wbuf[h][z, ylo, core, :, lanes] = kw[:, h * HD:(h + 1) * HD]
    pl.semaphore_wait(barrier, len(peers + near))

    sent = []
    outs = []

    def send(src, dst, ssem, rsem, at):
        copy = pltpu.make_async_remote_copy(
            src_ref=src, dst_ref=dst, send_sem=ssem, recv_sem=rsem, device_id=device(*at), device_id_type=MESH)
        copy.start()
        sent.append(copy)

    def arrived(dst, ssem, rsem):
        pltpu.make_async_remote_copy(
            src_ref=dst, dst_ref=dst, send_sem=ssem, recv_sem=rsem, device_id=device(x, y, z, 1 - core),
            device_id_type=MESH).wait_recv()

    def slab(h, zz, yl):
        return wbuf[h].at[(zz + 2 * Z) % Z, yl, core]

    def ring(h, way, step):
        way_z = -sgn if way == 0 else sgn
        block = slab(h, z + way_z * step, ylo)
        if step > 0:
            arrived(block, z_send.at[h, way, step - 1], z_recv.at[h, way, step - 1])
        if step < (4 if way == 0 else 3):
            send(block, block, z_send.at[h, way, step], z_recv.at[h, way, step], (x, y, z - way_z, core))
        if step > (0 if h in ALL_Y else 1):
            send(block, block, y_send.at[h, way, step - 1], y_recv.at[h, way, step - 1], (x, y - way_z, z, core))

    def halves(h, zz, yl):
        block = slab(h, zz, yl)
        return block.at[pl.ds(0, rows // 2)], block.at[pl.ds(rows // 2, rows // 2)]

    def cross(h):
        low, high = halves(h, z, ylo)
        send(low, low, h_send.at[h, 0], h_recv.at[h, 0], (x, y + 1, z, core))
        send(high, high, h_send.at[h, 1], h_recv.at[h, 1], (x, y - 1, z, core))

    def crossed(h):
        low, high = halves(h, z, 1 - ylo)
        arrived(low, h_send.at[h, 0], h_recv.at[h, 0])
        arrived(high, h_send.at[h, 1], h_recv.at[h, 1])
        if h not in ALL_Y:
            block = slab(h, z, 1 - ylo)
            send(block, block, o_send.at[h, 0], o_recv.at[h, 0], (x, y, z + 1, core))
            send(block, block, o_send.at[h, 1], o_recv.at[h, 1], (x, y, z - 1, core))

    def share_own(h):
        own = wbuf[h].at[:, ylo, core]
        send(own, own, d_send.at[h, 0], d_recv.at[h, 0], (x, y, z, 1 - core))

    def share_other(h):
        if h not in ALL_Y:
            arrived(slab(h, z - 1, 1 - ylo), o_send.at[h, 0], o_recv.at[h, 0])
            arrived(slab(h, z + 1, 1 - ylo), o_send.at[h, 1], o_recv.at[h, 1])
        for way in (0, 1):
            way_z = -sgn if way == 0 else sgn
            for k in range(0 if h in ALL_Y else 1, 4 - way):
                arrived(slab(h, z + way_z * (k + 1), 1 - ylo), y_send.at[h, way, k], y_recv.at[h, way, k])
        own = wbuf[h].at[:, 1 - ylo, core]
        send(own, own, d_send.at[h, 1], d_recv.at[h, 1], (x, y, z, 1 - core))

    def kv_send_to(h, n, block, at):
        send(block, block, kv_send.at[h, n], kv_recv.at[h, n], at)

    def kv_arrived(h, n, block):
        arrived(block, kv_send.at[h, n], kv_recv.at[h, n])

    def project(h):
        arrived(wbuf[h].at[:, ylo, 1 - core], d_send.at[h, 0], d_recv.at[h, 0])
        arrived(wbuf[h].at[:, 1 - ylo, 1 - core], d_send.at[h, 1], d_recv.at[h, 1])
        width = wbuf[h].shape[-1]
        weight = wbuf[h][...].reshape(normed.shape[1], width)
        sums = jnp.dot(normed[...], weight, preferred_element_type=jnp.float32)
        made = []
        if h > 0:
            made.append(sums[:, :HD].astype(jnp.bfloat16))
        if h < KVH:
            raw = sums[:, width - HD:]
            normk = raw * lax.rsqrt(jnp.mean(raw * raw, axis=-1, keepdims=True) + EPS) * key_gain_ref[...]
            turned = jnp.concatenate([normk[:, HD // 2:], normk[:, :HD // 2]], axis=1)
            made.append((normk * cos[...] + turned * sin[...]).astype(jnp.bfloat16))
        both = jnp.concatenate(made, axis=1)
        kv[h][ctx] = jnp.dot(perm[...], both, preferred_element_type=jnp.float32).astype(jnp.bfloat16)
        block = kv[h].at[ctx]
        kv_send_to(h, 0, block, (x, y + 2, z, core))
        kv_send_to(h, 1, block, (x + 1, y, z, core))
        kv_send_to(h, 2, block, (x - 1, y, z, core))

    def spread(h, yh, base, side):
        step = 1 if side == 0 else -1
        block = kv[h].at[((x - step + X) % X) * 2 + yh]
        kv_arrived(h, base + side, block)
        if base == 1 or h not in BY_Y:
            part = block.at[pl.ds(side * half, half)]
            kv_send_to(h, base + 2 + side, part, (x + step, y, z, core))

    def kv_partner(h):
        other = kv[h].at[x * 2 + 1 - yhi]
        kv_arrived(h, 0, other)
        kv_send_to(h, 5, other, (x + 1, y, z, core))
        kv_send_to(h, 6, other, (x - 1, y, z, core))

    def far(h, yh):
        return kv[h].at[((x + 2) % X) * 2 + yh]

    def kv_far(h):
        for side in (0, 1):
            kv_arrived(h, 3 + side, far(h, yhi).at[pl.ds(side * half, half)])
        if h in BY_Y:
            kv_send_to(h, 9, far(h, yhi), (x, y + 2, z, core))

    def kv_last(h):
        if h in BY_Y:
            kv_arrived(h, 9, far(h, 1 - yhi))
        else:
            for side in (0, 1):
                kv_arrived(h, 7 + side, far(h, 1 - yhi).at[pl.ds(side * half, half)])

    def order():
        shape = (tokens, tokens)
        down, across = lax.broadcasted_iota(jnp.int32, shape, 0), lax.broadcasted_iota(jnp.int32, shape, 1)
        same = down == across

        def column(row):
            return jnp.sum(jnp.where(same, row, 0.0), axis=1, keepdims=True)

        for load in loads[2:5]:
            load.wait()
        where = position_ref[...].astype(jnp.float32)
        row = (segment_ref[...] * BIG + position_ref[...]).astype(jnp.float32)
        col = column(row)
        rank_row = jnp.sum(jnp.where(col < row, 1.0, 0.0), axis=0, keepdims=True)
        rank_col = jnp.sum(jnp.where(row < col, 1.0, 0.0), axis=1, keepdims=True)
        put = rank_row == down.astype(jnp.float32)
        take = rank_col == across.astype(jnp.float32)
        perm[...] = jnp.where(put, 1.0, 0.0).astype(jnp.bfloat16)
        perm_t[...] = jnp.where(take, 1.0, 0.0).astype(jnp.bfloat16)
        codes[ctx] = jnp.sum(jnp.where(take, col, 0.0), axis=0, keepdims=True).astype(jnp.int32)
        own_code[...] = jnp.broadcast_to(jnp.sum(jnp.where(put, row, 0.0), axis=1, keepdims=True), (tokens, HD)).astype(jnp.int32)
        for n, at in enumerate(peers):
            send(codes.at[ctx], codes.at[ctx], c_send.at[n], c_recv.at[n], at)
        lane = lax.broadcasted_iota(jnp.int32, (1, HD), 1)
        freq = jnp.exp((lane % (HD // 2)).astype(jnp.float32) * (-2.0 * math.log(THETA) / HD))
        angle = column(where) * freq
        cos[...] = jnp.cos(angle)
        sin[...] = jnp.where(lane < HD // 2, -1.0, 1.0) * jnp.sin(angle)

    def masks():
        for n in range(len(peers)):
            dx, dy = [(dx, dy) for dx in range(X) for dy in (0, 2) if (dx, dy) != (0, 0)][n]
            src = ((x + X - dx) % X) * 2 + (yhi + dy // 2) % 2
            arrived(codes.at[src], c_send.at[n], c_recv.at[n])
        own = own_code[:, :1]
        start = own // BIG * BIG
        for j in range(TILES):
            there = jnp.concatenate([codes[d, :, j * slots:(j + 1) * slots] for d in range(GROUPS)], axis=1)
            bias[j] = jnp.where((there <= own) & (there >= start), jnp.float32(3e38), jnp.float32(NEG))

    def sort_queries():
        loads[7].wait()
        for h in range(KVH):
            part = pl.ds(h * G * HD, G * HD)
            queries[:, part] = jnp.dot(perm[...], queries[:, part], preferred_element_type=jnp.float32).astype(jnp.bfloat16)

    def block_of(i, j):
        return i * (i + 1) // 2 + j

    def tiles(n, i, lanes):
        parts = [kv[n][:, j * slots:(j + 1) * slots, lanes].reshape(keys_in, HD) for j in range(i + 1)]
        return jnp.concatenate(parts, axis=0)

    def scores(h, i):
        blk = queries[i * slots:(i + 1) * slots, h * G * HD:(h + 1) * G * HD]
        q = jnp.concatenate([blk[:, g * HD:(g + 1) * HD] for g in range(G)], axis=0)
        keys = tiles(h, i, slice(0, HD) if h == 0 else slice(HD, 2 * HD))
        s = lax.dot_general(q, keys, (((1,), (1,)), ((), ())), preferred_element_type=jnp.float32)
        top = None
        for j in range(i + 1):
            t = s[:, j * keys_in:(j + 1) * keys_in].reshape(G, slots, keys_in)
            t = jnp.minimum(t, bias[j, i * slots:(i + 1) * slots, :][None]).reshape(m, keys_in)
            held[block_of(i, j)] = t
            most = jnp.maximum(jnp.maximum(t[:, :HD], t[:, HD:2 * HD]), jnp.maximum(t[:, 2 * HD:3 * HD], t[:, 3 * HD:]))
            top = most if top is None else jnp.maximum(top, most)
        tops[i] = top

    def weigh(h, i):
        low = jnp.max(tops[i], axis=1, keepdims=True) * shift
        w = [jnp.exp2(held[block_of(i, j)] * shift - low).astype(jnp.bfloat16) for j in range(i + 1)]
        value = tiles(h + 1, i, slice(0, HD))
        value = jnp.concatenate([value, jnp.ones_like(value)], axis=1)
        acc = jnp.dot(jnp.concatenate(w, axis=1), value, preferred_element_type=jnp.float32)
        res = (acc[:, :HD] / acc[:, HD:]).astype(jnp.bfloat16)
        part = pl.ds(i * slots, slots)
        rows_out[part, :] = jnp.concatenate([res[g * slots:(g + 1) * slots] for g in range(G)], axis=1)
        if i == TILES - 1:
            out[h] = jnp.dot(perm_t[...], rows_out[...], preferred_element_type=jnp.float32).astype(jnp.bfloat16)
            copy = pltpu.make_async_copy(out.at[h], out_hbm.at[:, pl.ds(h * G * HD, G * HD)], out_sem.at[h])
            copy.start()
            outs.append(copy)

    def norm():
        loads[5].wait()
        loads[6].wait()

        @pl.loop(0, tokens // 32)
        def _(n):
            part = pl.ds(pl.multiple_of(n * 32, 32), 32)
            wide = hidden[part, :].astype(jnp.float32)
            scale = lax.rsqrt(jnp.mean(wide * wide, axis=-1, keepdims=True) + EPS)
            normed[part, :] = (wide * scale * gain_ref[...]).astype(jnp.bfloat16)

    steps = {
        "z": ring, "h": cross, "o": crossed, "E": share_own, "f": share_other, "p": project,
        "K": lambda h, side: spread(h, yhi, 1, side), "L": kv_partner,
        "M": lambda h, side: spread(h, 1 - yhi, 5, side), "Q": kv_far, "N": kv_last, "S": scores, "V": weigh,
    }
    plain = {"n": norm, "r": order, "m": masks, "q": sort_queries}
    for item in ORDER:
        if item in plain:
            plain[item]()
        else:
            steps[item[0]](*[int(digit) for digit in item[1:]])
    for copy in sent:
        copy.wait_send()
    for out in outs:
        out.wait()


def fused(hidden, queries, norm_gain, key_gain, segment, position, k_weight, v_weight):
    tokens, features = hidden.shape
    rows = k_weight.shape[0]
    slots = tokens // TILES
    m, keys_in = G * slots, GROUPS * slots
    hbm = pl.BlockSpec(memory_space=pl.ANY)
    dma = pltpu.SemaphoreType.DMA
    half, full = jnp.bfloat16, jnp.float32
    return pl.pallas_call(
        fused_kernel,
        out_shape=jax.ShapeDtypeStruct(queries.shape, half),
        in_specs=[hbm] * 8,
        out_specs=hbm,
        scratch_shapes=[
            pltpu.VMEM((tokens, features), half),
            pltpu.VMEM(queries.shape, half),
            pltpu.VMEM(norm_gain.shape, full),
            pltpu.VMEM(key_gain.shape, full),
            pltpu.VMEM(segment.shape, jnp.int32),
            pltpu.VMEM(position.shape, jnp.int32),
            pltpu.VMEM(k_weight.shape, half),
            pltpu.VMEM(v_weight.shape, half),
            pltpu.VMEM((2, Z, 2, 2, rows, HD), half),
            pltpu.VMEM((KVH - 1, Z, 2, 2, rows, 2 * HD), half),
            pltpu.VMEM((tokens, features), half),
            pltpu.VMEM((2, GROUPS, tokens, HD), half),
            pltpu.VMEM((KVH - 1, GROUPS, tokens, 2 * HD), half),
            pltpu.VMEM((GROUPS, 1, tokens), jnp.int32),
            pltpu.VMEM((tokens, tokens), half),
            pltpu.VMEM((tokens, tokens), half),
            pltpu.VMEM((tokens, HD), full),
            pltpu.VMEM((tokens, HD), full),
            pltpu.VMEM((tokens, HD), jnp.int32),
            pltpu.VMEM((TILES, tokens, keys_in), full),
            pltpu.VMEM((TILES * (TILES + 1) // 2, m, keys_in), full),
            pltpu.VMEM((TILES, m, HD), full),
            pltpu.VMEM((tokens, G * HD), half),
            pltpu.VMEM((KVH, tokens, G * HD), half),
            dma((8,)),
            dma((PARTS, 2, 4)), dma((PARTS, 2, 4)), dma((PARTS, 2)), dma((PARTS, 2)), dma((PARTS, 2)), dma((PARTS, 2)),
            dma((PARTS, 2, 4)), dma((PARTS, 2, 4)), dma((PARTS, 2)), dma((PARTS, 2)),
            dma((PARTS, 10)), dma((PARTS, 10)), dma((7,)), dma((7,)), dma((KVH,)),
        ],
        compiler_params=pltpu.CompilerParams(collective_id=0, has_side_effects=True, vmem_limit_bytes=60 * 2**20),
        cost_estimate=pl.CostEstimate(flops=12 * 10**9, bytes_accessed=10**8, transcendentals=2 * 10**7),
        name="project_gather_attend",
    )(hidden, queries, norm_gain, key_gain, segment, position, k_weight, v_weight)


def on_device(hidden, queries, norm_gain, key_gain, k_weight, v_weight, segment, position):
    return fused(hidden[0], queries[0], norm_gain[None], key_gain[None], segment, position, k_weight, v_weight)[None]


def solution(mesh):
    placed = (
        P("fsdp", "ctx", None),
        P("fsdp", "ctx", None),
        P(),
        P(),
        P("fsdp", None),
        P("fsdp", None),
        P("fsdp", "ctx"),
        P("fsdp", "ctx"),
    )
    return jax.shard_map(
        on_device, mesh=mesh, in_specs=placed, out_specs=P("fsdp", "ctx", None), check_vma=False
    )
```

```python
import functools
import math

import jax
import jax.numpy as jnp
from jax import lax
from jax.experimental import pallas as pl
from jax.experimental.pallas import tpu as pltpu
from jax.sharding import PartitionSpec as P

KVH = 4
HD = 128
G = 8
GROUPS = 8
EPS = 1e-06
THETA = 1000000.0
BIG = 8192
NEG = -1e30
X, Y, Z = 4, 4, 8
TILES = 4
MESH = pl.DeviceIdType.MESH


def place():
    f = lax.axis_index("fsdp")
    c = lax.axis_index("ctx")
    return c // 2, (c % 2) * 2 + (f // 2) % 2, f // 4, f % 2


def device(x, y, z, core):
    x, y, z = (x + X) % X, (y + Y) % Y, (z + Z) % Z
    return {"fsdp": (z * 2 + y % 2) * 2 + core, "ctx": x * 2 + y // 2}


ORDER = (
    "z000", "z210", "z010", "h4", "h0", "z100", "h1", "z310", "z300", "h3", "z001", "z110", "z200", "r", "h2",
    "z011", "z211", "z101", "z002", "n", "o1", "z111", "z410", "z201", "z102", "z003", "z112", "z012", "z202",
    "z103", "z301", "m", "z212", "z400", "q", "z311", "z004", "z411", "o0", "z113", "z013", "z203", "z104", "z312",
    "z302", "z401", "f0", "E0", "o2", "o3", "z412", "z213", "E1", "z204", "f1", "p0", "z303", "p1", "K00", "E2",
    "z402", "K01", "o4", "f2", "L0", "z304", "z403", "z313", "E3", "K11", "K10", "z413", "Q0", "L1", "p2", "f3",
    "z404", "Q1", "M00", "p3", "M01", "M10", "f4", "E4", "M11", "K20", "N0", "S01", "S02", "K21", "L2", "S00", "p4",
    "N1", "K31", "V00", "K30", "V01", "Q2", "S03", "L3", "V02", "V03", "S11", "S10", "M20", "S13", "S12", "L4",
    "K41", "M21", "Q3", "N2", "V10", "K40", "V11", "S21", "V12", "S22", "V13", "S23", "S20", "M31", "M41", "M30",
    "M40", "Q4", "N3", "V20", "V21", "S31", "V22", "S30", "V23", "S33", "S32", "N4", "V30", "V31", "V32", "V33",
)
PARTS = KVH + 1
BY_Y = (0, 1, 2, 3, 4)
ALL_Y = (0, 1)
DIRECT = ()


def fused_kernel(
    hidden_hbm, queries_hbm, gain_hbm, key_gain_hbm, segment_hbm, position_hbm, kw_hbm, vw_hbm,
    out_hbm,
    hidden, queries, gain_ref, key_gain_ref, segment_ref, position_ref, kw, vw, w_edge, w_mid, normed, kv_edge, kv_mid,
    codes, perm, perm_t, cos, sin, own_code, bias, held, tops, rows_out, out,
    in_sem, z_send, z_recv, o_send, o_recv, h_send, h_recv, y_send, y_recv, d_send, d_recv,
    kv_send, kv_recv, c_send, c_recv, out_sem,
):
    x, y, z, core = place()
    ylo, yhi = y % 2, y // 2
    ctx = x * 2 + yhi
    sgn = 1 - 2 * core
    rows = kw.shape[0]
    wbuf = [w_edge.at[0]] + [w_mid.at[n] for n in range(KVH - 1)] + [w_edge.at[1]]
    kv = [kv_edge.at[0]] + [kv_mid.at[n] for n in range(KVH - 1)] + [kv_edge.at[1]]
    tokens = hidden.shape[0]
    half = tokens // 2
    slots = tokens // TILES
    m, keys_in = G * slots, GROUPS * slots
    shift = math.log2(math.e) / math.sqrt(HD)

    loads = [pltpu.make_async_copy(a, b, in_sem.at[n]) for n, (a, b) in enumerate(((kw_hbm, kw), (vw_hbm, vw), (segment_hbm, segment_ref), (position_hbm, position_ref), (key_gain_hbm, key_gain_ref), (gain_hbm, gain_ref), (hidden_hbm, hidden), (queries_hbm, queries)))]
    for load in loads:
        load.start()
    ways = [(dx, 0) for dx in (1, -1, 2)] + [(dx, 2) for dx in (0, 1, -1, 2)]
    peers = [(x + dx, y + dy, z, core) for dx, dy in ways]
    origins = [((x - dx + X) % X) * 2 + (yhi + dy // 2) % 2 for dx, dy in ways]
    near = [(x, y, z + 1, core), (x, y, z - 1, core), (x, y + 1, z, core), (x, y - 1, z, core), (x, y, z, 1 - core)]
    barrier = pltpu.get_barrier_semaphore()
    for at in near + peers:
        pl.semaphore_signal(barrier, inc=1, device_id=device(*at), device_id_type=MESH)
    loads[0].wait()
    loads[1].wait()
    for h in range(PARTS):
        if h > 0:
            wbuf[h][z, ylo, core, :, :HD] = vw[:, (h - 1) * HD:h * HD]
        if h < KVH:
            lanes = slice(0, HD) if h == 0 else slice(HD, 2 * HD)
            wbuf[h][z, ylo, core, :, lanes] = kw[:, h * HD:(h + 1) * HD]
    pl.semaphore_wait(barrier, len(peers + near))

    sent = []
    outs = []

    def send(src, dst, ssem, rsem, at):
        copy = pltpu.make_async_remote_copy(
            src_ref=src, dst_ref=dst, send_sem=ssem, recv_sem=rsem, device_id=device(*at), device_id_type=MESH)
        copy.start()
        sent.append(copy)

    def arrived(dst, ssem, rsem):
        pltpu.make_async_remote_copy(
            src_ref=dst, dst_ref=dst, send_sem=ssem, recv_sem=rsem, device_id=device(x, y, z, 1 - core),
            device_id_type=MESH).wait_recv()

    def slab(h, zz, yl):
        return wbuf[h].at[(zz + 2 * Z) % Z, yl, core]

    def ring(h, way, step):
        way_z = -sgn if way == 0 else sgn
        block = slab(h, z + way_z * step, ylo)
        if step > 0:
            arrived(block, z_send.at[h, way, step - 1], z_recv.at[h, way, step - 1])
        if step < (4 if way == 0 else 3):
            send(block, block, z_send.at[h, way, step], z_recv.at[h, way, step], (x, y, z - way_z, core))
        if step > (0 if h in ALL_Y else 1):
            send(block, block, y_send.at[h, way, step - 1], y_recv.at[h, way, step - 1], (x, y - way_z, z, core))

    def halves(h, zz, yl):
        block = slab(h, zz, yl)
        return block.at[pl.ds(0, rows // 2)], block.at[pl.ds(rows // 2, rows // 2)]

    def cross(h):
        low, high = halves(h, z, ylo)
        send(low, low, h_send.at[h, 0], h_recv.at[h, 0], (x, y + 1, z, core))
        send(high, high, h_send.at[h, 1], h_recv.at[h, 1], (x, y - 1, z, core))

    def crossed(h):
        low, high = halves(h, z, 1 - ylo)
        arrived(low, h_send.at[h, 0], h_recv.at[h, 0])
        arrived(high, h_send.at[h, 1], h_recv.at[h, 1])
        if h not in ALL_Y:
            block = slab(h, z, 1 - ylo)
            send(block, block, o_send.at[h, 0], o_recv.at[h, 0], (x, y, z + 1, core))
            send(block, block, o_send.at[h, 1], o_recv.at[h, 1], (x, y, z - 1, core))

    def share_own(h):
        own = wbuf[h].at[:, ylo, core]
        send(own, own, d_send.at[h, 0], d_recv.at[h, 0], (x, y, z, 1 - core))

    def share_other(h):
        if h not in ALL_Y:
            arrived(slab(h, z - 1, 1 - ylo), o_send.at[h, 0], o_recv.at[h, 0])
            arrived(slab(h, z + 1, 1 - ylo), o_send.at[h, 1], o_recv.at[h, 1])
        for way in (0, 1):
            way_z = -sgn if way == 0 else sgn
            for k in range(0 if h in ALL_Y else 1, 4 - way):
                arrived(slab(h, z + way_z * (k + 1), 1 - ylo), y_send.at[h, way, k], y_recv.at[h, way, k])
        own = wbuf[h].at[:, 1 - ylo, core]
        send(own, own, d_send.at[h, 1], d_recv.at[h, 1], (x, y, z, 1 - core))

    def kv_send_to(h, n, block, at):
        send(block, block, kv_send.at[h, n], kv_recv.at[h, n], at)

    def kv_arrived(h, n, block):
        arrived(block, kv_send.at[h, n], kv_recv.at[h, n])

    def project(h):
        arrived(wbuf[h].at[:, ylo, 1 - core], d_send.at[h, 0], d_recv.at[h, 0])
        arrived(wbuf[h].at[:, 1 - ylo, 1 - core], d_send.at[h, 1], d_recv.at[h, 1])
        width = wbuf[h].shape[-1]
        weight = wbuf[h][...].reshape(normed.shape[1], width)
        sums = jnp.dot(normed[...], weight, preferred_element_type=jnp.float32)
        made = []
        if h > 0:
            made.append(sums[:, :HD].astype(jnp.bfloat16))
        if h < KVH:
            raw = sums[:, width - HD:]
            normk = raw * lax.rsqrt(jnp.mean(raw * raw, axis=-1, keepdims=True) + EPS) * key_gain_ref[...]
            turned = jnp.concatenate([normk[:, HD // 2:], normk[:, :HD // 2]], axis=1)
            made.append((normk * cos[...] + turned * sin[...]).astype(jnp.bfloat16))
        both = jnp.concatenate(made, axis=1)
        kv[h][ctx] = jnp.dot(perm[...], both, preferred_element_type=jnp.float32).astype(jnp.bfloat16)
        block = kv[h].at[ctx]
        if h in DIRECT:
            for n in reversed(range(len(peers))):
                kv_send_to(h, n, block, peers[n])
            return
        kv_send_to(h, 0, block, (x, y + 2, z, core))
        kv_send_to(h, 1, block, (x + 1, y, z, core))
        kv_send_to(h, 2, block, (x - 1, y, z, core))

    def spread(h, yh, base, side):
        step = 1 if side == 0 else -1
        block = kv[h].at[((x - step + X) % X) * 2 + yh]
        kv_arrived(h, base + side, block)
        if base == 1 or h not in BY_Y:
            part = block.at[pl.ds(side * half, half)]
            kv_send_to(h, base + 2 + side, part, (x + step, y, z, core))

    def kv_partner(h):
        other = kv[h].at[x * 2 + 1 - yhi]
        kv_arrived(h, 0, other)
        kv_send_to(h, 5, other, (x + 1, y, z, core))
        kv_send_to(h, 6, other, (x - 1, y, z, core))

    def far(h, yh):
        return kv[h].at[((x + 2) % X) * 2 + yh]

    def kv_far(h):
        for side in (0, 1):
            kv_arrived(h, 3 + side, far(h, yhi).at[pl.ds(side * half, half)])
        if h in BY_Y:
            kv_send_to(h, 9, far(h, yhi), (x, y + 2, z, core))

    def kv_last(h):
        if h in DIRECT:
            for n, origin in enumerate(origins):
                kv_arrived(h, n, kv[h].at[origin])
            return
        if h in BY_Y:
            kv_arrived(h, 9, far(h, 1 - yhi))
        else:
            for side in (0, 1):
                kv_arrived(h, 7 + side, far(h, 1 - yhi).at[pl.ds(side * half, half)])

    def order():
        shape = (tokens, tokens)
        down, across = lax.broadcasted_iota(jnp.int32, shape, 0), lax.broadcasted_iota(jnp.int32, shape, 1)
        same = down == across

        def column(row):
            return jnp.sum(jnp.where(same, row, 0.0), axis=1, keepdims=True)

        for load in loads[2:5]:
            load.wait()
        where = position_ref[...].astype(jnp.float32)
        row = (segment_ref[...] * BIG + position_ref[...]).astype(jnp.float32)
        col = column(row)
        rank_row = jnp.sum(jnp.where(col < row, 1.0, 0.0), axis=0, keepdims=True)
        rank_col = jnp.sum(jnp.where(row < col, 1.0, 0.0), axis=1, keepdims=True)
        put = rank_row == down.astype(jnp.float32)
        take = rank_col == across.astype(jnp.float32)
        perm[...] = jnp.where(put, 1.0, 0.0).astype(jnp.bfloat16)
        perm_t[...] = jnp.where(take, 1.0, 0.0).astype(jnp.bfloat16)
        codes[ctx] = jnp.sum(jnp.where(take, col, 0.0), axis=0, keepdims=True).astype(jnp.int32)
        own_code[...] = jnp.broadcast_to(jnp.sum(jnp.where(put, row, 0.0), axis=1, keepdims=True), (tokens, HD)).astype(jnp.int32)
        for n, at in enumerate(peers):
            send(codes.at[ctx], codes.at[ctx], c_send.at[n], c_recv.at[n], at)
        lane = lax.broadcasted_iota(jnp.int32, (1, HD), 1)
        freq = jnp.exp((lane % (HD // 2)).astype(jnp.float32) * (-2.0 * math.log(THETA) / HD))
        angle = column(where) * freq
        cos[...] = jnp.cos(angle)
        sin[...] = jnp.where(lane < HD // 2, -1.0, 1.0) * jnp.sin(angle)

    def masks():
        for n, origin in enumerate(origins):
            arrived(codes.at[origin], c_send.at[n], c_recv.at[n])
        own = own_code[:, :1]
        start = own // BIG * BIG
        for j in range(TILES):
            there = jnp.concatenate([codes[d, :, j * slots:(j + 1) * slots] for d in range(GROUPS)], axis=1)
            bias[j] = jnp.where((there <= own) & (there >= start), jnp.float32(3e38), jnp.float32(NEG))

    def sort_queries():
        loads[7].wait()
        for h in range(KVH):
            part = pl.ds(h * G * HD, G * HD)
            queries[:, part] = jnp.dot(perm[...], queries[:, part], preferred_element_type=jnp.float32).astype(jnp.bfloat16)

    def block_of(i, j):
        return i * (i + 1) // 2 + j

    def tiles(n, i, lanes):
        parts = [kv[n][:, j * slots:(j + 1) * slots, lanes].reshape(keys_in, HD) for j in range(i + 1)]
        return jnp.concatenate(parts, axis=0)

    def scores(h, i):
        blk = queries[i * slots:(i + 1) * slots, h * G * HD:(h + 1) * G * HD]
        q = jnp.concatenate([blk[:, g * HD:(g + 1) * HD] for g in range(G)], axis=0)
        keys = tiles(h, i, slice(0, HD) if h == 0 else slice(HD, 2 * HD))
        s = lax.dot_general(q, keys, (((1,), (1,)), ((), ())), preferred_element_type=jnp.float32)
        top = None
        for j in range(i + 1):
            t = s[:, j * keys_in:(j + 1) * keys_in].reshape(G, slots, keys_in)
            t = jnp.minimum(t, bias[j, i * slots:(i + 1) * slots, :][None]).reshape(m, keys_in)
            held[block_of(i, j)] = t
            most = jnp.maximum(jnp.maximum(t[:, :HD], t[:, HD:2 * HD]), jnp.maximum(t[:, 2 * HD:3 * HD], t[:, 3 * HD:]))
            top = most if top is None else jnp.maximum(top, most)
        tops[i] = top

    def weigh(h, i):
        low = jnp.max(tops[i], axis=1, keepdims=True) * shift
        w = [jnp.exp2(held[block_of(i, j)] * shift - low).astype(jnp.bfloat16) for j in range(i + 1)]
        value = tiles(h + 1, i, slice(0, HD))
        value = jnp.concatenate([value, jnp.ones_like(value)], axis=1)
        acc = jnp.dot(jnp.concatenate(w, axis=1), value, preferred_element_type=jnp.float32)
        res = (acc[:, :HD] / acc[:, HD:]).astype(jnp.bfloat16)
        part = pl.ds(i * slots, slots)
        rows_out[part, :] = jnp.concatenate([res[g * slots:(g + 1) * slots] for g in range(G)], axis=1)
        if i == TILES - 1:
            out[h] = jnp.dot(perm_t[...], rows_out[...], preferred_element_type=jnp.float32).astype(jnp.bfloat16)
            copy = pltpu.make_async_copy(out.at[h], out_hbm.at[:, pl.ds(h * G * HD, G * HD)], out_sem.at[h])
            copy.start()
            outs.append(copy)

    def norm():
        loads[5].wait()
        loads[6].wait()

        @pl.loop(0, tokens // 32)
        def _(n):
            part = pl.ds(pl.multiple_of(n * 32, 32), 32)
            wide = hidden[part, :].astype(jnp.float32)
            scale = lax.rsqrt(jnp.mean(wide * wide, axis=-1, keepdims=True) + EPS)
            normed[part, :] = (wide * scale * gain_ref[...]).astype(jnp.bfloat16)

    steps = {
        "z": ring, "h": cross, "o": crossed, "E": share_own, "f": share_other, "p": project,
        "K": lambda h, side: spread(h, yhi, 1, side), "L": kv_partner,
        "M": lambda h, side: spread(h, 1 - yhi, 5, side), "Q": kv_far, "N": kv_last, "S": scores, "V": weigh,
    }
    plain = {"n": norm, "r": order, "m": masks, "q": sort_queries}
    for item in ORDER:
        if item in plain:
            plain[item]()
        elif item[0] not in "KLMQ" or int(item[1]) not in DIRECT:
            steps[item[0]](*[int(digit) for digit in item[1:]])
    for copy in sent:
        copy.wait_send()
    for out in outs:
        out.wait()


def fused(hidden, queries, norm_gain, key_gain, segment, position, k_weight, v_weight):
    tokens, features = hidden.shape
    rows = k_weight.shape[0]
    slots = tokens // TILES
    m, keys_in = G * slots, GROUPS * slots
    hbm = pl.BlockSpec(memory_space=pl.ANY)
    dma = pltpu.SemaphoreType.DMA
    half, full = jnp.bfloat16, jnp.float32
    return pl.pallas_call(
        fused_kernel,
        out_shape=jax.ShapeDtypeStruct(queries.shape, half),
        in_specs=[hbm] * 8,
        out_specs=hbm,
        scratch_shapes=[
            pltpu.VMEM((tokens, features), half),
            pltpu.VMEM(queries.shape, half),
            pltpu.VMEM(norm_gain.shape, full),
            pltpu.VMEM(key_gain.shape, full),
            pltpu.VMEM(segment.shape, jnp.int32),
            pltpu.VMEM(position.shape, jnp.int32),
            pltpu.VMEM(k_weight.shape, half),
            pltpu.VMEM(v_weight.shape, half),
            pltpu.VMEM((2, Z, 2, 2, rows, HD), half),
            pltpu.VMEM((KVH - 1, Z, 2, 2, rows, 2 * HD), half),
            pltpu.VMEM((tokens, features), half),
            pltpu.VMEM((2, GROUPS, tokens, HD), half),
            pltpu.VMEM((KVH - 1, GROUPS, tokens, 2 * HD), half),
            pltpu.VMEM((GROUPS, 1, tokens), jnp.int32),
            pltpu.VMEM((tokens, tokens), half),
            pltpu.VMEM((tokens, tokens), half),
            pltpu.VMEM((tokens, HD), full),
            pltpu.VMEM((tokens, HD), full),
            pltpu.VMEM((tokens, HD), jnp.int32),
            pltpu.VMEM((TILES, tokens, keys_in), full),
            pltpu.VMEM((TILES * (TILES + 1) // 2, m, keys_in), full),
            pltpu.VMEM((TILES, m, HD), full),
            pltpu.VMEM((tokens, G * HD), half),
            pltpu.VMEM((KVH, tokens, G * HD), half),
            dma((8,)),
            dma((PARTS, 2, 4)), dma((PARTS, 2, 4)), dma((PARTS, 2)), dma((PARTS, 2)), dma((PARTS, 2)), dma((PARTS, 2)),
            dma((PARTS, 2, 4)), dma((PARTS, 2, 4)), dma((PARTS, 2)), dma((PARTS, 2)),
            dma((PARTS, 10)), dma((PARTS, 10)), dma((7,)), dma((7,)), dma((KVH,)),
        ],
        compiler_params=pltpu.CompilerParams(collective_id=0, has_side_effects=True, vmem_limit_bytes=60 * 2**20),
        cost_estimate=pl.CostEstimate(flops=12 * 10**9, bytes_accessed=10**8, transcendentals=2 * 10**7),
        name="project_gather_attend",
    )(hidden, queries, norm_gain, key_gain, segment, position, k_weight, v_weight)


def on_device(hidden, queries, norm_gain, key_gain, k_weight, v_weight, segment, position):
    return fused(hidden[0], queries[0], norm_gain[None], key_gain[None], segment, position, k_weight, v_weight)[None]


def solution(mesh):
    placed = (
        P("fsdp", "ctx", None),
        P("fsdp", "ctx", None),
        P(),
        P(),
        P("fsdp", None),
        P("fsdp", None),
        P("fsdp", "ctx"),
        P("fsdp", "ctx"),
    )
    return jax.shard_map(
        on_device, mesh=mesh, in_specs=placed, out_specs=P("fsdp", "ctx", None), check_vma=False
    )
```
